256 devices in a mesh: blk: 128 (over x, y, z), ch: 2 (over core).
Axes of the slice: x: 4, y: 4, z: 8, core: 2. Of those that a mesh axis runs over, the one named last changes fastest.
Arguments:
- blocks: float32 [8, 128, 256, 256], P(None, 'blk', None, 'ch'), may hold values from -1 to 5, as said below
Outputs:
- factor: float32 [4, 8, 128, 256, 256], P(None, None, 'blk', None, 'ch')
- second_row: float32 [8, 128, 256, 256], P(None, 'blk', None, 'ch')
The draws below stay inside these ranges and needn't reach their ends.
Inputs may be any that keep to these rules, and one draw needn't show every extreme that they name: blocks[0, 0] is symmetric, and the block-Toeplitz matrix built from the first 5 block columns is positive definite.
All inputs are finite; a program needn't handle non-finite values. Where the reference program divides by a largest or mean magnitude, that divisor is 1e-20 or more.
Results may differ from the reference program's by a relative error of at most 0.0003.
Values sent between devices are 32-bit elements; how exact they have to be, the bound alone decides.
A program may use at most 64 MiB of HBM per device.

```python
import math
import jax
import jax.numpy as jnp
from jax import lax

M = 256
BDEV = 8
STEPS = 3
N_BLK = 128


def draw_blocks(key, part):
    first_key, second_key = jax.random.split(key)
    base = jnp.clip(jax.random.normal(first_key, (BDEV, N_BLK, M, M), jnp.float32), -6.0, 6.0)
    square = jnp.clip(jax.random.normal(second_key, (M, M), jnp.float32), -6.0, 6.0)
    others = base * (0.2 / math.sqrt(M))
    noise = 0.4 * (square + square.T) / math.sqrt(2.0 * M)
    leading = 3.0 * jnp.eye(M, dtype=jnp.float32) + noise
    return others.at[0, 0].set(leading)


def setup_inputs(seed: int = 0) -> dict:
    streams_of = jax.random.split(jax.random.key(seed), 2)
    return {
        "blocks": draw_blocks(jax.random.fold_in(streams_of[1], 71), 0),
    }


def matmul(left, right):
    return jnp.dot(left, right, precision=lax.Precision.HIGHEST)

def root_inverse(matrix, sweeps):
    identity = jnp.eye(matrix.shape[0], dtype=matrix.dtype)
    scaling = jnp.max(lax.optimization_barrier(jnp.sum(jnp.abs(matrix), axis=1)))
    approach = matrix / scaling
    inv_part = identity
    for sweep_index in range(sweeps):
        middle = 1.5 * identity - 0.5 * matmul(inv_part, approach)
        approach = matmul(approach, middle)
        inv_part = matmul(middle, inv_part)
    return inv_part / jnp.sqrt(scaling)

def inverse_newton(matrix, sweeps):
    identity = jnp.eye(matrix.shape[0], dtype=matrix.dtype)
    scaling = jnp.max(lax.optimization_barrier(jnp.sum(jnp.abs(matrix), axis=1)))
    guess = identity / scaling
    for sweep_index in range(sweeps):
        guess = matmul(guess, 2.0 * identity - matmul(matrix, guess))
    return guess

def make_rotation(lead_upper, lead_second):
    width = lead_upper.shape[0]
    identity = jnp.eye(width, dtype=lead_upper.dtype)
    gram = matmul(lead_upper, lead_upper.T)
    cross = matmul(lead_upper, lead_second.T)
    coupling_t = matmul(inverse_newton(gram, 5), cross)
    coupling = coupling_t.T
    first_inv = root_inverse(identity - matmul(coupling_t, coupling), 5)
    second_inv = root_inverse(identity - matmul(coupling, coupling_t), 5)
    top_rows = jnp.concatenate([first_inv, -matmul(first_inv, coupling_t)], axis=1)
    bottom_rows = jnp.concatenate([-matmul(second_inv, coupling), second_inv], axis=1)
    return jnp.concatenate([top_rows, bottom_rows], axis=0)

def reference(blocks):
    flat = blocks.reshape(BDEV * N_BLK, M, M)
    first_inv = root_inverse(flat[0], 6)
    upper_row = jnp.einsum('ab,jbc->jac', first_inv, flat, precision=lax.Precision.HIGHEST)
    empty_block = jnp.zeros((1, M, M), dtype=flat.dtype)
    lower_row = jnp.concatenate([upper_row[1:], empty_block], axis=0)
    collected = [upper_row]
    for step_index in range(STEPS):
        rotation = make_rotation(upper_row[0], lower_row[0])
        joined = jnp.concatenate([upper_row, lower_row], axis=1)
        moved = jnp.einsum('ab,jbc->jac', rotation, joined, precision=lax.Precision.HIGHEST)
        upper_row = moved[:, :M]
        lower_row = moved[:, M:]
        collected.append(upper_row)
        lower_row = jnp.concatenate([lower_row[1:], empty_block], axis=0)
    factor = jnp.stack(collected).reshape(STEPS + 1, BDEV, N_BLK, M, M)
    return (factor, lower_row.reshape(BDEV, N_BLK, M, M))
```

```python
import functools

import jax
import jax.numpy as jnp
from jax import lax
from jax.experimental import pallas as pl
from jax.experimental.pallas import tpu as pltpu
from jax.sharding import PartitionSpec as P

MESH = pl.DeviceIdType.MESH
F32, BF16 = jnp.float32, jnp.bfloat16

STEPS = 3
LEADS = STEPS + 1
REACH = STEPS + 1
DEPTH = 8
DOWN = 5
FAR = 5


def split(a):
    high = a.astype(BF16)
    return high, (a - high.astype(F32)).astype(BF16)


def dot_of_parts(left, right):
    (lh, ll), (rh, rl) = left, right
    return jnp.dot(
        jnp.concatenate([lh, ll, lh], axis=1),
        jnp.concatenate([rh, rh, rl], axis=0),
        preferred_element_type=F32,
    )


def mul(left, right):
    return dot_of_parts(split(left), split(right))


def wait_for(ref, sem):
    pltpu.make_async_copy(ref, ref, sem).wait()


def kernel(n, depth, x_ref, factor_ref, second_ref, halo, lead, why, zed, stage, coef_high, coef_low, a_ref, c_ref,
           scatter_send, z_send, piece_recv, plane_send, plane_recv, sib_send, sib_recv,
           down_send, down_recv, up_send, up_recv, out_sem):
    width = x_ref.shape[1]
    count = x_ref.shape[0]
    half = x_ref.shape[2]
    ups = count - DOWN
    b, ch = lax.axis_index("blk"), lax.axis_index("ch")
    planes = n // depth
    rows = width // planes
    p, z = lax.div(b, depth), lax.rem(b, depth)
    below, above, far_below = lax.rem(b + n - 1, n), lax.rem(b + 1, n), lax.rem(b + n - FAR, n)

    def in_plane(i):
        return {"blk": lax.rem(p + i, planes) * depth + z}

    def in_line(i):
        return {"blk": p * depth + lax.rem(z + i, depth)}

    sibling = {"ch": 1 - ch}

    def each(start, stop, body):
        def run(i, carry):
            body(i)
            return carry

        lax.fori_loop(start, stop, run, 0)

    def push(src, dst, send, recv, to):
        return pltpu.make_async_remote_copy(
            src_ref=src, dst_ref=dst, send_sem=send, recv_sem=recv, device_id=to, device_id_type=MESH
        )

    barrier = pltpu.get_barrier_semaphore()

    def greet(to):
        pl.semaphore_signal(barrier, inc=1, device_id=to, device_id_type=MESH)

    for by in (1, n - 1, FAR, n - FAR):
        greet({"blk": lax.rem(b + by, n)})
    greet(sibling)
    each(1, planes, lambda i: greet(in_plane(i)))
    each(1, depth, lambda i: greet(in_line(i)))
    pl.semaphore_wait(barrier, 4 + 1 + (planes - 1) + (depth - 1))

    def piece(item, i):
        return lead.at[item, ch, pl.ds(pl.multiple_of(i * rows, rows), rows)]

    def own_piece(i):
        return x_ref.at[0, pl.ds(pl.multiple_of(i * rows, rows), rows)]

    def scatter_copy(i):
        return push(own_piece(i), piece(b, i), scatter_send.at[i], piece_recv.at[b], {"blk": i * depth + b})

    def line_copy(item, i):
        return push(piece(item, p), piece(item, p), z_send.at[i], piece_recv.at[item], in_line(i))

    def plane_copy(item, i):
        return push(piece(item, p), piece(item, p), plane_send.at[item, i], plane_recv.at[item], in_plane(i))

    def sibling_copy(item):
        return push(lead.at[item, ch], lead.at[item, ch], sib_send.at[item], sib_recv.at[item], sibling)

    @pl.when(b < LEADS)
    def _():
        pltpu.make_async_copy(own_piece(0), piece(b, 0), piece_recv.at[b]).start()
        each(1, planes, lambda i: scatter_copy(i).start())

    def down_copy(t, src):
        s, r = lax.div(t, DOWN), lax.rem(t, DOWN)
        return push(src, halo.at[s, r], down_send.at[t], down_recv.at[t], {"blk": below})

    def up_copy(t, src, to):
        s, r = FAR - 1 - lax.div(t, ups), DOWN + lax.rem(t, ups)
        return push(src, halo.at[s, r], up_send.at[t], up_recv.at[t], {"blk": to})

    def down_source(t):
        return halo.at[lax.div(t, DOWN) - 1, lax.rem(t, DOWN)]

    def up_source(t):
        return halo.at[FAR - lax.div(t, ups), DOWN + lax.rem(t, ups)]

    n_down, n_up = REACH * DOWN, (REACH + 1) * ups

    def down_arrived(t):
        wait_for(halo.at[lax.div(t, DOWN), lax.rem(t, DOWN)], down_recv.at[t])

    def up_arrived(t):
        wait_for(halo.at[FAR - 1 - lax.div(t, ups), DOWN + lax.rem(t, ups)], up_recv.at[t])

    def relay(t):
        @pl.when(t < n_down - DOWN)
        def _():
            down_arrived(t)
            down_copy(t + DOWN, down_source(t + DOWN)).start()

        @pl.when(t < n_up - ups)
        def _():
            up_arrived(t)
            up_copy(t + ups, up_source(t + ups), above).start()

    each(0, ups, lambda t: up_copy(t, x_ref.at[DOWN + t], far_below).start())
    each(0, 1, lambda t: down_copy(t, x_ref.at[t]).start())

    def pass_piece(item):
        wait_for(piece(item, p), piece_recv.at[item])

        @pl.when(z == item)
        def _():
            each(1, depth, lambda i: line_copy(item, i).start())

        each(1, planes, lambda i: plane_copy(item, i).start())

    each(0, LEADS, pass_piece)
    each(1, DOWN, lambda t: down_copy(t, x_ref.at[t]).start())

    def gathered(item):
        if planes > 1:
            wait_for(lead.at[item, ch, pl.ds(0, (planes - 1) * rows)], plane_recv.at[item])
        sibling_copy(item).start()

    def complete(item):
        wait_for(lead.at[item, 1 - ch], sib_recv.at[item])

    def lead_block(item):
        return jnp.concatenate([lead[item, 0], lead[item, 1]], axis=1)

    eye = (
        lax.broadcasted_iota(jnp.int32, (width, width), 0) == lax.broadcasted_iota(jnp.int32, (width, width), 1)
    ).astype(F32)

    def scale_of(a):
        return jnp.max(jnp.sum(jnp.abs(a), axis=0, keepdims=True), axis=1, keepdims=True)

    def roots(matrices, sweeps, first_tick):
        kept = range(len(matrices))
        scales = [scale_of(a) for a in matrices]
        starts = [a * (1.0 / s) for a, s in zip(matrices, scales)]
        middles = [1.5 * eye - 0.5 * y for y in starts]
        firsts = [mul(y, t) for y, t in zip(starts, middles)]
        for i in kept:
            zed[i] = middles[i]
            why[i] = firsts[i]

        def sweep(k, carry):
            relay(first_tick + k)
            ys = [split(why[i]) for i in kept]
            zs = [split(zed[i]) for i in kept]
            ts = [split(1.5 * eye - 0.5 * dot_of_parts(zs[i], ys[i])) for i in kept]
            new_ys = [dot_of_parts(ys[i], ts[i]) for i in kept]
            new_zs = [dot_of_parts(ts[i], zs[i]) for i in kept]
            for i in kept:
                why[i] = new_ys[i]
                zed[i] = new_zs[i]
            return carry

        lax.fori_loop(0, sweeps - 1, sweep, 0)
        return scales

    def cols(j, k=1):
        return pl.ds(j * width, k * width)

    def keep_coefficients(o, value, terms):
        high, low = split(value)
        coef_high[o, :, : terms * width] = high
        coef_low[o, :, : terms * width] = low

    gathered(0)
    complete(0)
    (s,) = roots([lead_block(0)], 6, 0)
    root = jnp.sqrt(s)
    w = zed[0] * (1.0 / root)
    x0 = why[0] * root
    for item in range(1, LEADS):
        gathered(item)
    for item in range(1, LEADS):
        complete(item)
    rest = mul(w, jnp.concatenate([lead_block(item) for item in range(1, LEADS)], axis=1))
    uppers = [x0] + [rest[:, i * width : (i + 1) * width] for i in range(LEADS - 1)]
    lowers = uppers[1:]
    keep_coefficients(0, w, 1)
    a_ref[:, cols(0)] = w
    c_ref[:, cols(0)] = w
    tick = 5

    for k in range(STEPS):
        terms = k + 1
        x, y = uppers[0], lowers[0]
        both = mul(x, jnp.concatenate([x.T, y.T], axis=1))
        gram, cross = both[:, :width], both[:, width:]
        s = 1.0 / scale_of(gram)
        power = eye - gram * s
        total = cross * s
        for i in range(4):
            both = mul(power, jnp.concatenate([power, total], axis=1))
            power, total = both[:, :width], total + both[:, width:]
        kt = total + mul(power, total)
        kk = kt.T
        kt_parts, kk_parts = split(kt), split(kk)
        scales = roots([eye - dot_of_parts(kt_parts, kk_parts), eye - dot_of_parts(kk_parts, kt_parts)], 5, tick)
        tick += 4
        first = zed[0] * (1.0 / jnp.sqrt(scales[0]))
        second = zed[1] * (1.0 / jnp.sqrt(scales[1]))
        first_parts, second_parts = split(first), split(second)
        more = STEPS - 1 - k
        if more > 0:
            d = jnp.concatenate(uppers[:more], axis=1) - dot_of_parts(
                kt_parts, split(jnp.concatenate(lowers[:more], axis=1)))
            e = jnp.concatenate(lowers[1 : more + 1], axis=1) - dot_of_parts(
                kk_parts, split(jnp.concatenate(uppers[1 : more + 1], axis=1)))
            d = dot_of_parts(first_parts, split(d))
            e = dot_of_parts(second_parts, split(e))
            uppers = [d[:, i * width : (i + 1) * width] for i in range(more)]
            lowers = [e[:, i * width : (i + 1) * width] for i in range(more)]
        a, c = a_ref[:, cols(0, terms)], c_ref[:, cols(0, terms)]
        ktc = dot_of_parts(kt_parts, split(c))
        kka = dot_of_parts(kk_parts, split(a))
        none = jnp.zeros((width, width), F32)
        d = jnp.concatenate([a, none], axis=1) - jnp.concatenate([none, ktc], axis=1)
        e = jnp.concatenate([none, c], axis=1) - jnp.concatenate([kka, none], axis=1)
        a = dot_of_parts(first_parts, split(d))
        c = dot_of_parts(second_parts, split(e))
        a_ref[:, cols(0, terms + 1)] = a
        c_ref[:, cols(0, terms + 1)] = c
        keep_coefficients(k + 1, a, terms + 1)
        if k == STEPS - 1:
            keep_coefficients(STEPS + 1, c, terms + 1)

    def data(j, q):
        wrapped = (b + j >= n).astype(jnp.int32)
        blocks = []
        for i in range(2):
            r = 2 * q + i
            if j == 0:
                blocks.append(x_ref[r])
            else:
                block = halo[j - 1, jnp.minimum(r + wrapped, count - 1)]
                blocks.append(jnp.where(r + wrapped < count, block, jnp.zeros_like(block)))
        return split(jnp.concatenate(blocks, axis=1))

    def out_copy(o, q):
        target = factor_ref.at[o, pl.ds(2 * q, 2)] if o <= STEPS else second_ref.at[pl.ds(2 * q, 2)]
        return pltpu.make_async_copy(stage.at[o, pl.ds(2 * q, 2)], target, out_sem.at[o, q])

    def emit(o, q, parts):
        terms = len(parts)
        high, low = coef_high[o, :, : terms * width], coef_low[o, :, : terms * width]
        rh = jnp.concatenate([part[0] for part in parts], axis=0)
        rl = jnp.concatenate([part[1] for part in parts], axis=0)
        value = dot_of_parts((high, low), (rh, rl))
        stage[o, 2 * q] = value[:, :half]
        stage[o, 2 * q + 1] = value[:, half:]
        out_copy(o, q).start()

    def emit_pair(q, outputs):
        last = REACH if STEPS + 1 in outputs else max(outputs)
        parts = [data(j, q) for j in range(last + 1)]
        for o in outputs:
            emit(o, q, parts[: o + 1] if o <= STEPS else parts[1:])

    each(0, 4, lambda q: emit_pair(q, [0]))
    each(0, 2, lambda q: emit_pair(q, [1, 2, 3]))
    each(n_down - DOWN, n_down, down_arrived)
    each(0, 2, lambda q: emit_pair(q, [4]))
    each(n_up - ups, n_up, up_arrived)
    each(2, 4, lambda q: emit_pair(q, [1, 2, 3, 4]))

    @pl.when(b < LEADS)
    def _():
        each(1, planes, lambda i: scatter_copy(i).wait_send())
        each(1, depth, lambda i: line_copy(b, i).wait_send())

    @pl.when((b >= LEADS) & (z < LEADS))
    def _():
        each(1, depth, lambda i: line_copy(z, i).wait_send())

    for item in range(LEADS):
        each(1, planes, lambda i: plane_copy(item, i).wait_send())
        sibling_copy(item).wait_send()
    each(0, n_down, lambda t: down_copy(t, x_ref.at[0]).wait_send())
    each(0, n_up, lambda t: up_copy(t, x_ref.at[0], above).wait_send())
    for o in range(STEPS + 2):
        each(0, 4, lambda q: out_copy(o, q).wait())


def body(n, depth, blocks):
    local = blocks[:, 0]
    count, width, half = local.shape
    ups = count - DOWN
    planes = n // depth
    dma = pltpu.SemaphoreType.DMA
    any_space = pl.BlockSpec(memory_space=pl.ANY)
    factor, second = pl.pallas_call(
        functools.partial(kernel, n, depth),
        out_shape=(
            jax.ShapeDtypeStruct((STEPS + 1, count, width, half), F32),
            jax.ShapeDtypeStruct((count, width, half), F32),
        ),
        in_specs=[pl.BlockSpec(memory_space=pltpu.VMEM)],
        out_specs=(any_space, any_space),
        scratch_shapes=[
            pltpu.VMEM((FAR, count, width, half), F32),
            pltpu.VMEM((LEADS, 2, width, half), F32),
            pltpu.VMEM((2, width, width), F32),
            pltpu.VMEM((2, width, width), F32),
            pltpu.VMEM((STEPS + 2, count, width, half), F32),
            pltpu.VMEM((STEPS + 2, width, (STEPS + 1) * width), BF16),
            pltpu.VMEM((STEPS + 2, width, (STEPS + 1) * width), BF16),
            pltpu.VMEM((width, (STEPS + 1) * width), F32),
            pltpu.VMEM((width, (STEPS + 1) * width), F32),
            dma((planes,)),
            dma((depth,)),
            dma((LEADS,)),
            dma((LEADS, planes)),
            dma((LEADS,)),
            dma((LEADS,)),
            dma((LEADS,)),
            dma((REACH * DOWN,)),
            dma((REACH * DOWN,)),
            dma(((REACH + 1) * ups,)),
            dma(((REACH + 1) * ups,)),
            dma((STEPS + 2, 4)),
        ],
        compiler_params=pltpu.CompilerParams(
            collective_id=0, has_side_effects=True, vmem_limit_bytes=48 * 1024 * 1024
        ),
        cost_estimate=pl.CostEstimate(flops=20_000_000_000, bytes_accessed=6 * 1024 * 1024, transcendentals=0),
    )(local)
    return factor[:, :, None], second[:, None]


def solution(mesh, depth=DEPTH):
    n = mesh.shape["blk"]
    return jax.shard_map(
        functools.partial(body, n, depth),
        mesh=mesh,
        in_specs=(P(None, "blk", None, "ch"),),
        out_specs=(P(None, None, "blk", None, "ch"), P(None, "blk", None, "ch")),
        check_vma=False,
    )
```

```python
import functools

import jax
import jax.numpy as jnp
from jax import lax
from jax.experimental import pallas as pl
from jax.experimental.pallas import tpu as pltpu
from jax.sharding import PartitionSpec as P

MESH = pl.DeviceIdType.MESH
F32, BF16 = jnp.float32, jnp.bfloat16

STEPS = 3
OWN_AT = (([0, 1, 2], [0]), ([3, 4], [1, 2]), ([], []), ([], []))
AT_START = (([], []), ([10], [4]), ([13], [7]))
AFTER_INVERSE = (([8], [2]), ([11], [5]), ([14], [8]))
AFTER_ROOTS = (([9], [3]), ([12], [6]), ([], [9]))
LEADS = STEPS + 1
REACH = STEPS + 1
DEPTH = 8
SIDE = 4
DOWN = 5
FAR = REACH + 1
RISE = 3


def split(a):
    high = a.astype(BF16)
    return high, (a - high.astype(F32)).astype(BF16)


def dot_of_parts(left, right):
    (lh, ll), (rh, rl) = left, right
    return jnp.dot(
        jnp.concatenate([lh, ll, lh], axis=1),
        jnp.concatenate([rh, rh, rl], axis=0),
        preferred_element_type=F32,
    )


def mul(left, right):
    return dot_of_parts(split(left), split(right))


def wait_for(ref, sem):
    pltpu.make_async_copy(ref, ref, sem).wait()


def kernel(n, depth, side, x_ref, factor_ref, second_ref, halo, lead, why, zed, coef_high, coef_low, a_ref, c_ref,
           scatter_send, z_send, piece_recv, y_send, y_recv, row_send, row_recv, sib_send, sib_recv,
           down_send, down_recv, up_send, up_recv):
    width = x_ref.shape[1]
    count = x_ref.shape[0]
    half = x_ref.shape[2]
    ups = count - DOWN
    b, ch = lax.axis_index("blk"), lax.axis_index("ch")
    planes = n // depth
    rows = width // planes
    p, z = lax.div(b, depth), lax.rem(b, depth)
    below, above = lax.rem(b + n - 1, n), lax.rem(b + 1, n)
    first_stop = p * depth + lax.rem(z + RISE, depth)
    held_from = p * depth + lax.rem(z + depth - RISE, depth)
    second_stop = lax.rem(held_from + n - REACH, n)
    sender = lax.rem(b + REACH, n)
    second_sender = lax.div(sender, depth) * depth + lax.rem(lax.rem(sender, depth) + RISE, depth)

    across = planes // side
    row, column = lax.div(p, side), lax.rem(p, side)

    def in_row(i):
        return {"blk": (row * side + lax.rem(column + i, side)) * depth + z}

    def in_column(i):
        return {"blk": (lax.rem(row + i, across) * side + column) * depth + z}

    def in_line(i):
        return {"blk": p * depth + lax.rem(z + i, depth)}

    sibling = {"ch": 1 - ch}

    def each(start, stop, body):
        def run(i, carry):
            body(i)
            return carry

        lax.fori_loop(start, stop, run, 0)

    def push(src, dst, send, recv, to):
        return pltpu.make_async_remote_copy(
            src_ref=src, dst_ref=dst, send_sem=send, recv_sem=recv, device_id=to, device_id_type=MESH
        )

    barrier = pltpu.get_barrier_semaphore()

    def greet(to):
        pl.semaphore_signal(barrier, inc=1, device_id=to, device_id_type=MESH)

    for to in (above, below, held_from, second_sender):
        greet({"blk": to})
    greet(sibling)
    for i in range(1, side):
        greet(in_row(i))
    for i in range(1, across):
        greet(in_column(i))
    for item in range(LEADS):

        @pl.when(z != item)
        def _():
            greet({"blk": p * depth + item})

    @pl.when((z < LEADS) & (p > 0))
    def _():
        greet({"blk": z})

    owner, forwards = (b < LEADS).astype(jnp.int32), (z < LEADS).astype(jnp.int32)
    pl.semaphore_wait(
        barrier, 5 + (side - 1) + (across - 1) + forwards * (depth - 1) + owner * (planes - 1)
    )

    def piece(item, i):
        return lead.at[item, ch, pl.ds(pl.multiple_of(i * rows, rows), rows)]

    def own_piece(i):
        return x_ref.at[0, pl.ds(pl.multiple_of(i * rows, rows), rows)]

    def scatter_copy(i):
        return push(own_piece(i), piece(b, i), scatter_send.at[i], piece_recv.at[b], {"blk": i * depth + b})

    def line_copy(item, i):
        return push(piece(item, p), piece(item, p), z_send.at[i], piece_recv.at[item], in_line(i))

    groups = ((0, 1), (1, LEADS - 1))

    def lead_rows(g, start, size):
        return lead.at[pl.ds(*groups[g]), ch, pl.ds(start, size)]

    def ring(g, size, place, region, neighbour, sends, recvs):
        def copy(k, part, by):
            return push(region(g, part), region(g, part), sends.at[g, k], recvs.at[g, k], neighbour(by))

        before, after = lax.rem(place + size - 1, size), lax.rem(place + 1, size)
        copies = [copy(0, place, 1), copy(1, place, size - 1), copy(2, before, 1)][: size - 1]

        def first():
            for c in copies[:2]:
                c.start()

        def second():
            if size > 1:
                wait_for(region(g, before), recvs.at[g, 0])
            if size > 3:
                copies[2].start()

        def third():
            if size > 2:
                wait_for(region(g, after), recvs.at[g, 1])
            if size > 3:
                wait_for(region(g, lax.rem(place + 2, size)), recvs.at[g, 2])

        def sent():
            for c in copies:
                c.wait_send()

        return first, second, third, sent

    def row_region(g, i):
        return lead_rows(g, pl.multiple_of((row * side + i) * rows, rows), rows)

    def column_region(g, i):
        return lead_rows(g, pl.multiple_of(i * side * rows, side * rows), side * rows)

    row_rings = [ring(g, side, column, row_region, in_row, y_send, y_recv) for g in range(2)]
    column_rings = [ring(g, across, row, column_region, in_column, row_send, row_recv) for g in range(2)]

    def sibling_copy(g):
        part = lead.at[pl.ds(*groups[g]), ch]
        return push(part, part, sib_send.at[g], sib_recv.at[g], sibling)

    def complete(g):
        wait_for(lead.at[pl.ds(*groups[g]), 1 - ch], sib_recv.at[g])

    @pl.when(b < LEADS)
    def _():
        pltpu.make_async_copy(own_piece(0), piece(b, 0), piece_recv.at[b]).start()
        each(1, planes, lambda i: scatter_copy(i).start())

    def down_copy(t, src):
        s, r = lax.div(t, DOWN), lax.rem(t, DOWN)
        return push(src, halo.at[s, r], down_send.at[t], down_recv.at[t], {"blk": below})

    def up_copy(t, src, to):
        s, r = FAR - 1 - lax.div(t, ups), DOWN + lax.rem(t, ups)
        return push(src, halo.at[s, r], up_send.at[t], up_recv.at[t], {"blk": to})

    def down_source(t):
        return halo.at[lax.div(t, DOWN) - 1, lax.rem(t, DOWN)]

    def up_source(t):
        return halo.at[FAR - lax.div(t, ups), DOWN + lax.rem(t, ups)]

    n_down, n_up = REACH * DOWN, (REACH + 1) * ups

    def down_arrived(t):
        wait_for(halo.at[lax.div(t, DOWN), lax.rem(t, DOWN)], down_recv.at[t])

    def up_arrived(t):
        wait_for(halo.at[FAR - 1 - lax.div(t, ups), DOWN + lax.rem(t, ups)], up_recv.at[t])

    def relay(downs=(), upwards=()):
        for t in downs:
            down_arrived(t)
            down_copy(t + DOWN, down_source(t + DOWN)).start()
        for t in upwards:
            up_arrived(t)
            up_copy(t + ups, up_source(t + ups), second_stop if t < ups else above).start()

    def own(downs=(), upwards=()):
        for t in downs:
            down_copy(t, x_ref.at[t]).start()
        for t in upwards:
            up_copy(t, x_ref.at[DOWN + t], first_stop).start()

    def pass_pieces(g):
        first, size = groups[g]
        for item in range(first, first + size):

            @pl.when(z != item)
            def _():
                wait_for(piece(item, p), piece_recv.at[item])

        row_rings[g][0]()

    own(*OWN_AT[0])

    @pl.when(z < LEADS)
    def _():
        wait_for(piece(z, p), piece_recv.at[z])
        each(1, depth, lambda i: line_copy(z, i).start())

    own(*OWN_AT[1])
    pass_pieces(0)
    pass_pieces(1)
    own(*OWN_AT[2])
    row_rings[0][1]()
    row_rings[1][1]()
    for g in range(2):
        row_rings[g][2]()
        column_rings[g][0]()
    own(*OWN_AT[3])
    column_rings[0][1]()
    column_rings[1][1]()
    relay([0, 1])
    column_rings[0][2]()
    sibling_copy(0).start()
    relay([2])
    column_rings[1][2]()
    sibling_copy(1).start()
    relay([3])

    def lead_block(item):
        return jnp.concatenate([lead[item, 0], lead[item, 1]], axis=1)

    eye = (
        lax.broadcasted_iota(jnp.int32, (width, width), 0) == lax.broadcasted_iota(jnp.int32, (width, width), 1)
    ).astype(F32)

    def scale_of(a):
        return jnp.max(jnp.sum(jnp.abs(a), axis=0, keepdims=True), axis=1, keepdims=True)

    def roots(matrices, sweeps):
        kept = range(len(matrices))
        scales = [scale_of(a) for a in matrices]
        starts = [a * (1.0 / s) for a, s in zip(matrices, scales)]
        middles = [1.5 * eye - 0.5 * y for y in starts]
        firsts = [mul(y, t) for y, t in zip(starts, middles)]
        for i in kept:
            zed[i] = middles[i]
            why[i] = firsts[i]

        def sweep(k, carry):
            ys = [split(why[i]) for i in kept]
            zs = [split(zed[i]) for i in kept]
            ts = [split(1.5 * eye - 0.5 * dot_of_parts(zs[i], ys[i])) for i in kept]
            new_ys = [dot_of_parts(ys[i], ts[i]) for i in kept]
            new_zs = [dot_of_parts(ts[i], zs[i]) for i in kept]
            for i in kept:
                why[i] = new_ys[i]
                zed[i] = new_zs[i]
            return carry

        lax.fori_loop(0, sweeps - 1, sweep, 0)
        return scales

    def cols(j, k=1):
        return pl.ds(j * width, k * width)

    def keep_coefficients(o, value, terms):
        high, low = split(value)
        coef_high[o, :, : terms * width] = high
        coef_low[o, :, : terms * width] = low

    complete(0)
    relay([4])
    (s,) = roots([lead_block(0)], 6)
    relay([5, 6], [0])
    root = jnp.sqrt(s)
    w = zed[0] * (1.0 / root)
    x0 = why[0] * root
    complete(1)
    rest = mul(w, jnp.concatenate([lead_block(item) for item in range(1, LEADS)], axis=1))
    uppers = [x0] + [rest[:, i * width : (i + 1) * width] for i in range(LEADS - 1)]
    lowers = uppers[1:]
    keep_coefficients(0, w, 1)
    a_ref[:, cols(0)] = w
    c_ref[:, cols(0)] = w
    relay([7], [1])

    for k in range(STEPS):
        terms = k + 1
        x, y = uppers[0], lowers[0]
        relay(*AT_START[k])
        both = mul(x, jnp.concatenate([x.T, y.T], axis=1))
        gram, cross = both[:, :width], both[:, width:]
        s = 1.0 / scale_of(gram)
        power = eye - gram * s
        total = cross * s
        for i in range(4):
            both = mul(power, jnp.concatenate([power, total], axis=1))
            power, total = both[:, :width], total + both[:, width:]
        kt = total + mul(power, total)
        kk = kt.T
        kt_parts, kk_parts = split(kt), split(kk)
        relay(*AFTER_INVERSE[k])
        scales = roots([eye - dot_of_parts(kt_parts, kk_parts), eye - dot_of_parts(kk_parts, kt_parts)], 5)
        relay(*AFTER_ROOTS[k])
        first = zed[0] * (1.0 / jnp.sqrt(scales[0]))
        second = zed[1] * (1.0 / jnp.sqrt(scales[1]))
        first_parts, second_parts = split(first), split(second)
        more = STEPS - 1 - k
        if more > 0:
            d = jnp.concatenate(uppers[:more], axis=1) - dot_of_parts(
                kt_parts, split(jnp.concatenate(lowers[:more], axis=1)))
            e = jnp.concatenate(lowers[1 : more + 1], axis=1) - dot_of_parts(
                kk_parts, split(jnp.concatenate(uppers[1 : more + 1], axis=1)))
            d = dot_of_parts(first_parts, split(d))
            e = dot_of_parts(second_parts, split(e))
            uppers = [d[:, i * width : (i + 1) * width] for i in range(more)]
            lowers = [e[:, i * width : (i + 1) * width] for i in range(more)]
        a, c = a_ref[:, cols(0, terms)], c_ref[:, cols(0, terms)]
        ktc = dot_of_parts(kt_parts, split(c))
        kka = dot_of_parts(kk_parts, split(a))
        none = jnp.zeros((width, width), F32)
        d = jnp.concatenate([a, none], axis=1) - jnp.concatenate([none, ktc], axis=1)
        e = jnp.concatenate([none, c], axis=1) - jnp.concatenate([kka, none], axis=1)
        a = dot_of_parts(first_parts, split(d))
        c = dot_of_parts(second_parts, split(e))
        a_ref[:, cols(0, terms + 1)] = a
        c_ref[:, cols(0, terms + 1)] = c
        keep_coefficients(k + 1, a, terms + 1)
        if k == STEPS - 1:
            keep_coefficients(STEPS + 1, c, terms + 1)

    def data(j, q):
        wrapped = (b + j >= n).astype(jnp.int32)
        blocks = []
        for i in range(2):
            r = 2 * q + i
            if j == 0:
                blocks.append(x_ref[r])
            else:
                block = halo[j - 1, jnp.minimum(r + wrapped, count - 1)]
                blocks.append(jnp.where(r + wrapped < count, block, jnp.zeros_like(block)))
        return split(jnp.concatenate(blocks, axis=1))

    def terms_of(o, q, slots, add):
        shift = 1 if o > STEPS else 0
        parts = [data(j, q) for j in slots]
        left = [
            jnp.concatenate([ref[o, :, (j - shift) * width : (j - shift + 1) * width] for j in slots], axis=1)
            for ref in (coef_high, coef_low)
        ]
        right = [jnp.concatenate([part[i] for part in parts], axis=0) for i in range(2)]
        value = dot_of_parts(left, right)
        for i in range(2):
            cut = value[:, i * half : (i + 1) * half]
            r = 2 * q + i
            if o > STEPS:
                second_ref[r] = second_ref[r] + cut if add else cut
            else:
                factor_ref[o, r] = factor_ref[o, r] + cut if add else cut

    def own_row(q):
        terms_of(0, q, [0], False)

    def near_rows(q):
        for o in range(1, STEPS + 1):
            terms_of(o, q, list(range(o + 1)), False)
        terms_of(STEPS + 1, q, [1, 2, 3], False)

    def near_last(q):
        terms_of(STEPS + 1, q, [4], True)

    def far_rows(q, row):
        terms_of(2, q, [0, 2], False)
        terms_of(3, q, [0, 2, 3], False)
        terms_of(4, q, row, False)

    def far_last(q, row):
        terms_of(1, q, [0, 1], False)
        for o in range(2, STEPS + 1):
            terms_of(o, q, [1], True)
        terms_of(STEPS + 1, q, row, True)

    relay([], [10])
    each(0, 4, own_row)
    relay([], [11])
    each(0, 2, near_rows)
    far_rows(2, [2, 3])
    far_rows(3, [2, 3, 4])
    each(n_down - DOWN, n_down, down_arrived)
    each(0, 2, near_last)
    each(n_up - ups, n_up, up_arrived)
    far_last(2, [1, 4])
    far_last(3, [1])

    @pl.when(b < LEADS)
    def _():
        each(1, planes, lambda i: scatter_copy(i).wait_send())
        each(1, depth, lambda i: line_copy(b, i).wait_send())

    @pl.when((b >= LEADS) & (z < LEADS))
    def _():
        each(1, depth, lambda i: line_copy(z, i).wait_send())

    for g in range(len(groups)):
        row_rings[g][3]()
        column_rings[g][3]()
        sibling_copy(g).wait_send()
    each(0, n_down, lambda t: down_copy(t, x_ref.at[0]).wait_send())
    each(0, n_up, lambda t: up_copy(t, x_ref.at[0], above).wait_send())


def body(n, depth, side, blocks):
    local = blocks[:, 0]
    count, width, half = local.shape
    ups = count - DOWN
    planes = n // depth
    dma = pltpu.SemaphoreType.DMA
    in_vmem = pl.BlockSpec(memory_space=pltpu.VMEM)
    factor, second = pl.pallas_call(
        functools.partial(kernel, n, depth, side),
        out_shape=(
            jax.ShapeDtypeStruct((STEPS + 1, count, width, half), F32),
            jax.ShapeDtypeStruct((count, width, half), F32),
        ),
        in_specs=[in_vmem],
        out_specs=(in_vmem, in_vmem),
        scratch_shapes=[
            pltpu.VMEM((FAR, count, width, half), F32),
            pltpu.VMEM((LEADS, 2, width, half), F32),
            pltpu.VMEM((2, width, width), F32),
            pltpu.VMEM((2, width, width), F32),
            pltpu.VMEM((STEPS + 2, width, (STEPS + 1) * width), BF16),
            pltpu.VMEM((STEPS + 2, width, (STEPS + 1) * width), BF16),
            pltpu.VMEM((width, (STEPS + 1) * width), F32),
            pltpu.VMEM((width, (STEPS + 1) * width), F32),
            dma((planes,)),
            dma((depth,)),
            dma((LEADS,)),
            dma((2, 3)),
            dma((2, 3)),
            dma((2, 3)),
            dma((2, 3)),
            dma((2,)),
            dma((2,)),
            dma((REACH * DOWN,)),
            dma((REACH * DOWN,)),
            dma(((REACH + 1) * ups,)),
            dma(((REACH + 1) * ups,)),
        ],
        compiler_params=pltpu.CompilerParams(
            collective_id=0, has_side_effects=True, vmem_limit_bytes=40 * 1024 * 1024
        ),
        cost_estimate=pl.CostEstimate(flops=20_000_000_000, bytes_accessed=6 * 1024 * 1024, transcendentals=0),
    )(local)
    return factor[:, :, None], second[:, None]


def solution(mesh, depth=DEPTH, side=SIDE):
    n = mesh.shape["blk"]
    return jax.shard_map(
        functools.partial(body, n, depth, side),
        mesh=mesh,
        in_specs=(P(None, "blk", None, "ch"),),
        out_specs=(P(None, None, "blk", None, "ch"), P(None, "blk", None, "ch")),
        check_vma=False,
    )
```

```python
import functools

import jax
import jax.numpy as jnp
from jax import lax
from jax.experimental import pallas as pl
from jax.experimental.pallas import tpu as pltpu
from jax.sharding import PartitionSpec as P

MESH = pl.DeviceIdType.MESH
F32, BF16 = jnp.float32, jnp.bfloat16

STEPS = 3
OWN_AT = (([0, 1, 2], [0]), ([3, 4], [1, 2]), ([], []), ([], []))
AT_START = (([], []), ([10], [4]), ([13], [7]))
AFTER_INVERSE = (([8], [2]), ([11], [5]), ([14], [8]))
AFTER_ROOTS = (([9], [3]), ([12], [6]), ([], [9]))
LEADS = STEPS + 1
REACH = STEPS + 1
DEPTH = 8
SIDE = 4
DOWN = 5
FAR = REACH + 1
RISE = 3


def split(a):
    high = a.astype(BF16)
    return high, (a - high.astype(F32)).astype(BF16)


def dot_of_parts(left, right):
    (lh, ll), (rh, rl) = left, right
    return jnp.dot(
        jnp.concatenate([lh, ll, lh], axis=1),
        jnp.concatenate([rh, rh, rl], axis=0),
        preferred_element_type=F32,
    )


def mul(left, right):
    return dot_of_parts(split(left), split(right))


def wait_for(ref, sem):
    pltpu.make_async_copy(ref, ref, sem).wait()


def kernel(n, depth, side, x_ref, factor_ref, second_ref, halo, lead, why, zed, coef_high, coef_low, a_ref, c_ref,
           scatter_send, z_send, piece_recv, y_send, y_recv, row_send, row_recv, sib_send, sib_recv,
           down_send, down_recv, up_send, up_recv):
    width = x_ref.shape[1]
    count = x_ref.shape[0]
    half = x_ref.shape[2]
    ups = count - DOWN
    b, ch = lax.axis_index("blk"), lax.axis_index("ch")
    planes = n // depth
    rows = width // planes
    p, z = lax.div(b, depth), lax.rem(b, depth)
    below, above = lax.rem(b + n - 1, n), lax.rem(b + 1, n)
    first_stop = p * depth + lax.rem(z + RISE, depth)
    held_from = p * depth + lax.rem(z + depth - RISE, depth)
    second_stop = lax.rem(held_from + n - REACH, n)
    sender = lax.rem(b + REACH, n)
    second_sender = lax.div(sender, depth) * depth + lax.rem(lax.rem(sender, depth) + RISE, depth)

    across = planes // side
    row, column = lax.div(p, side), lax.rem(p, side)

    def in_row(i):
        return {"blk": (row * side + lax.rem(column + i, side)) * depth + z}

    def in_column(i):
        return {"blk": (lax.rem(row + i, across) * side + column) * depth + z}

    def in_line(i):
        return {"blk": p * depth + lax.rem(z + i, depth)}

    sibling = {"ch": 1 - ch}

    def each(start, stop, body):
        def run(i, carry):
            body(i)
            return carry

        lax.fori_loop(start, stop, run, 0)

    def push(src, dst, send, recv, to):
        return pltpu.make_async_remote_copy(
            src_ref=src, dst_ref=dst, send_sem=send, recv_sem=recv, device_id=to, device_id_type=MESH
        )

    barrier = pltpu.get_barrier_semaphore()

    def greet(to):
        pl.semaphore_signal(barrier, inc=1, device_id=to, device_id_type=MESH)

    for to in (above, below, held_from, second_sender):
        greet({"blk": to})
    greet(sibling)
    for i in range(1, side):
        greet(in_row(i))
    for i in range(1, across):
        greet(in_column(i))
    for item in range(LEADS):

        @pl.when(z != item)
        def _():
            greet({"blk": p * depth + item})

    @pl.when((z < LEADS) & (p > 0))
    def _():
        greet({"blk": z})

    owner, forwards = (b < LEADS).astype(jnp.int32), (z < LEADS).astype(jnp.int32)
    pl.semaphore_wait(
        barrier, 5 + (side - 1) + (across - 1) + forwards * (depth - 1) + owner * (planes - 1)
    )

    def piece(item, i):
        return lead.at[item, ch, pl.ds(pl.multiple_of(i * rows, rows), rows)]

    def own_piece(i):
        return x_ref.at[0, pl.ds(pl.multiple_of(i * rows, rows), rows)]

    def scatter_copy(i):
        return push(own_piece(i), piece(b, i), scatter_send.at[i], piece_recv.at[b], {"blk": i * depth + b})

    def line_copy(item, i):
        return push(piece(item, p), piece(item, p), z_send.at[i], piece_recv.at[item], in_line(i))

    groups = ((0, 1), (1, LEADS - 1))

    def lead_rows(g, start, size):
        return lead.at[pl.ds(*groups[g]), ch, pl.ds(start, size)]

    def ring(g, size, place, region, neighbour, sends, recvs):
        def copy(k, part, by):
            return push(region(g, part), region(g, part), sends.at[g, k], recvs.at[g, k], neighbour(by))

        behind = [lax.rem(place + size - i, size) for i in range(size)]
        copies = [copy(i, behind[i], 1) for i in range(size - 1)]

        def first():
            for c in copies[:1]:
                c.start()

        def arrived(i):
            wait_for(region(g, behind[i]), recvs.at[g, i - 1])
            for c in copies[i : i + 1]:
                c.start()

        def second():
            if size > 1:
                arrived(1)

        def third():
            for i in range(2, size):
                arrived(i)

        def sent():
            for c in copies:
                c.wait_send()

        return first, second, third, sent

    def row_region(g, i):
        return lead_rows(g, pl.multiple_of((row * side + i) * rows, rows), rows)

    def column_region(g, i):
        return lead_rows(g, pl.multiple_of(i * side * rows, side * rows), side * rows)

    row_rings = [ring(g, side, column, row_region, in_row, y_send, y_recv) for g in range(2)]
    column_rings = [ring(g, across, row, column_region, in_column, row_send, row_recv) for g in range(2)]

    def sibling_copy(g):
        part = lead.at[pl.ds(*groups[g]), ch]
        return push(part, part, sib_send.at[g], sib_recv.at[g], sibling)

    def complete(g):
        wait_for(lead.at[pl.ds(*groups[g]), 1 - ch], sib_recv.at[g])

    @pl.when(b < LEADS)
    def _():
        pltpu.make_async_copy(own_piece(0), piece(b, 0), piece_recv.at[b]).start()
        each(1, planes, lambda i: scatter_copy(i).start())

    def down_copy(t, src):
        s, r = lax.div(t, DOWN), lax.rem(t, DOWN)
        return push(src, halo.at[s, r], down_send.at[t], down_recv.at[t], {"blk": below})

    def up_copy(t, src, to):
        s, r = FAR - 1 - lax.div(t, ups), DOWN + lax.rem(t, ups)
        return push(src, halo.at[s, r], up_send.at[t], up_recv.at[t], {"blk": to})

    def down_source(t):
        return halo.at[lax.div(t, DOWN) - 1, lax.rem(t, DOWN)]

    def up_source(t):
        return halo.at[FAR - lax.div(t, ups), DOWN + lax.rem(t, ups)]

    n_down, n_up = REACH * DOWN, (REACH + 1) * ups

    def down_arrived(t):
        wait_for(halo.at[lax.div(t, DOWN), lax.rem(t, DOWN)], down_recv.at[t])

    def up_arrived(t):
        wait_for(halo.at[FAR - 1 - lax.div(t, ups), DOWN + lax.rem(t, ups)], up_recv.at[t])

    def relay(downs=(), upwards=()):
        for t in downs:
            down_arrived(t)
            down_copy(t + DOWN, down_source(t + DOWN)).start()
        for t in upwards:
            up_arrived(t)
            up_copy(t + ups, up_source(t + ups), second_stop if t < ups else above).start()

    def own(downs=(), upwards=()):
        for t in downs:
            down_copy(t, x_ref.at[t]).start()
        for t in upwards:
            up_copy(t, x_ref.at[DOWN + t], first_stop).start()

    def pass_pieces(g):
        first, size = groups[g]
        for item in range(first, first + size):

            @pl.when(z != item)
            def _():
                wait_for(piece(item, p), piece_recv.at[item])

        row_rings[g][0]()

    own(*OWN_AT[0])

    @pl.when(z < LEADS)
    def _():
        wait_for(piece(z, p), piece_recv.at[z])
        each(1, depth, lambda i: line_copy(z, i).start())

    own(*OWN_AT[1])
    pass_pieces(0)
    pass_pieces(1)
    own(*OWN_AT[2])
    row_rings[0][1]()
    row_rings[1][1]()
    for g in range(2):
        row_rings[g][2]()
        column_rings[g][0]()
    own(*OWN_AT[3])
    column_rings[0][1]()
    column_rings[1][1]()
    relay([0, 1])
    column_rings[0][2]()
    sibling_copy(0).start()
    relay([2])
    column_rings[1][2]()
    sibling_copy(1).start()
    relay([3])

    def lead_block(item):
        return jnp.concatenate([lead[item, 0], lead[item, 1]], axis=1)

    eye = (
        lax.broadcasted_iota(jnp.int32, (width, width), 0) == lax.broadcasted_iota(jnp.int32, (width, width), 1)
    ).astype(F32)

    def scale_of(a):
        return jnp.max(jnp.sum(jnp.abs(a), axis=0, keepdims=True), axis=1, keepdims=True)

    def roots(matrices, sweeps):
        kept = range(len(matrices))
        scales = [scale_of(a) for a in matrices]
        starts = [a * (1.0 / s) for a, s in zip(matrices, scales)]
        middles = [1.5 * eye - 0.5 * y for y in starts]
        firsts = [mul(y, t) for y, t in zip(starts, middles)]
        for i in kept:
            zed[i] = middles[i]
            why[i] = firsts[i]

        def sweep(k, carry):
            ys = [split(why[i]) for i in kept]
            zs = [split(zed[i]) for i in kept]
            ts = [split(1.5 * eye - 0.5 * dot_of_parts(zs[i], ys[i])) for i in kept]
            new_ys = [dot_of_parts(ys[i], ts[i]) for i in kept]
            new_zs = [dot_of_parts(ts[i], zs[i]) for i in kept]
            for i in kept:
                why[i] = new_ys[i]
                zed[i] = new_zs[i]
            return carry

        lax.fori_loop(0, sweeps - 1, sweep, 0)
        return scales

    def cols(j, k=1):
        return pl.ds(j * width, k * width)

    def keep_coefficients(o, value, terms):
        high, low = split(value)
        coef_high[o, :, : terms * width] = high
        coef_low[o, :, : terms * width] = low

    complete(0)
    relay([4])
    (s,) = roots([lead_block(0)], 6)
    relay([5, 6], [0])
    root = jnp.sqrt(s)
    w = zed[0] * (1.0 / root)
    x0 = why[0] * root
    complete(1)
    rest = mul(w, jnp.concatenate([lead_block(item) for item in range(1, LEADS)], axis=1))
    uppers = [x0] + [rest[:, i * width : (i + 1) * width] for i in range(LEADS - 1)]
    lowers = uppers[1:]
    keep_coefficients(0, w, 1)
    a_ref[:, cols(0)] = w
    c_ref[:, cols(0)] = w
    relay([7], [1])

    for k in range(STEPS):
        terms = k + 1
        x, y = uppers[0], lowers[0]
        relay(*AT_START[k])
        both = mul(x, jnp.concatenate([x.T, y.T], axis=1))
        gram, cross = both[:, :width], both[:, width:]
        s = 1.0 / scale_of(gram)
        power = eye - gram * s
        total = cross * s
        for i in range(4):
            both = mul(power, jnp.concatenate([power, total], axis=1))
            power, total = both[:, :width], total + both[:, width:]
        kt = total + mul(power, total)
        kk = kt.T
        kt_parts, kk_parts = split(kt), split(kk)
        relay(*AFTER_INVERSE[k])
        scales = roots([eye - dot_of_parts(kt_parts, kk_parts), eye - dot_of_parts(kk_parts, kt_parts)], 5)
        relay(*AFTER_ROOTS[k])
        first = zed[0] * (1.0 / jnp.sqrt(scales[0]))
        second = zed[1] * (1.0 / jnp.sqrt(scales[1]))
        first_parts, second_parts = split(first), split(second)
        more = STEPS - 1 - k
        if more > 0:
            d = jnp.concatenate(uppers[:more], axis=1) - dot_of_parts(
                kt_parts, split(jnp.concatenate(lowers[:more], axis=1)))
            e = jnp.concatenate(lowers[1 : more + 1], axis=1) - dot_of_parts(
                kk_parts, split(jnp.concatenate(uppers[1 : more + 1], axis=1)))
            d = dot_of_parts(first_parts, split(d))
            e = dot_of_parts(second_parts, split(e))
            uppers = [d[:, i * width : (i + 1) * width] for i in range(more)]
            lowers = [e[:, i * width : (i + 1) * width] for i in range(more)]
        a, c = a_ref[:, cols(0, terms)], c_ref[:, cols(0, terms)]
        ktc = dot_of_parts(kt_parts, split(c))
        kka = dot_of_parts(kk_parts, split(a))
        none = jnp.zeros((width, width), F32)
        d = jnp.concatenate([a, none], axis=1) - jnp.concatenate([none, ktc], axis=1)
        e = jnp.concatenate([none, c], axis=1) - jnp.concatenate([kka, none], axis=1)
        a = dot_of_parts(first_parts, split(d))
        c = dot_of_parts(second_parts, split(e))
        a_ref[:, cols(0, terms + 1)] = a
        c_ref[:, cols(0, terms + 1)] = c
        keep_coefficients(k + 1, a, terms + 1)
        if k == STEPS - 1:
            keep_coefficients(STEPS + 1, c, terms + 1)

    def data(j, q):
        wrapped = (b + j >= n).astype(jnp.int32)
        blocks = []
        for i in range(2):
            r = 2 * q + i
            if j == 0:
                blocks.append(x_ref[r])
            else:
                block = halo[j - 1, jnp.minimum(r + wrapped, count - 1)]
                blocks.append(jnp.where(r + wrapped < count, block, jnp.zeros_like(block)))
        return split(jnp.concatenate(blocks, axis=1))

    def terms_of(o, q, slots, add):
        shift = 1 if o > STEPS else 0
        parts = [data(j, q) for j in slots]
        left = [
            jnp.concatenate([ref[o, :, (j - shift) * width : (j - shift + 1) * width] for j in slots], axis=1)
            for ref in (coef_high, coef_low)
        ]
        right = [jnp.concatenate([part[i] for part in parts], axis=0) for i in range(2)]
        value = dot_of_parts(left, right)
        for i in range(2):
            cut = value[:, i * half : (i + 1) * half]
            r = 2 * q + i
            if o > STEPS:
                second_ref[r] = second_ref[r] + cut if add else cut
            else:
                factor_ref[o, r] = factor_ref[o, r] + cut if add else cut

    def own_row(q):
        terms_of(0, q, [0], False)

    def near_rows(q):
        for o in range(1, STEPS + 1):
            terms_of(o, q, list(range(o + 1)), False)
        terms_of(STEPS + 1, q, [1, 2, 3], False)

    def near_last(q):
        terms_of(STEPS + 1, q, [4], True)

    def far_rows(q, row):
        terms_of(2, q, [0, 2], False)
        terms_of(3, q, [0, 2, 3], False)
        terms_of(4, q, row, False)

    def far_last(q, row):
        terms_of(1, q, [0, 1], False)
        for o in range(2, STEPS + 1):
            terms_of(o, q, [1], True)
        terms_of(STEPS + 1, q, row, True)

    relay([], [10])
    each(0, 4, own_row)
    relay([], [11])
    each(0, 2, near_rows)
    far_rows(2, [2, 3])
    far_rows(3, [2, 3, 4])
    each(n_down - DOWN, n_down, down_arrived)
    each(0, 2, near_last)
    each(n_up - ups, n_up, up_arrived)
    far_last(2, [1, 4])
    far_last(3, [1])

    @pl.when(b < LEADS)
    def _():
        each(1, planes, lambda i: scatter_copy(i).wait_send())
        each(1, depth, lambda i: line_copy(b, i).wait_send())

    @pl.when((b >= LEADS) & (z < LEADS))
    def _():
        each(1, depth, lambda i: line_copy(z, i).wait_send())

    for g in range(len(groups)):
        row_rings[g][3]()
        column_rings[g][3]()
        sibling_copy(g).wait_send()
    each(0, n_down, lambda t: down_copy(t, x_ref.at[0]).wait_send())
    each(0, n_up, lambda t: up_copy(t, x_ref.at[0], above).wait_send())


def body(n, depth, side, blocks):
    local = blocks[:, 0]
    count, width, half = local.shape
    ups = count - DOWN
    planes = n // depth
    dma = pltpu.SemaphoreType.DMA
    in_vmem = pl.BlockSpec(memory_space=pltpu.VMEM)
    factor, second = pl.pallas_call(
        functools.partial(kernel, n, depth, side),
        out_shape=(
            jax.ShapeDtypeStruct((STEPS + 1, count, width, half), F32),
            jax.ShapeDtypeStruct((count, width, half), F32),
        ),
        in_specs=[in_vmem],
        out_specs=(in_vmem, in_vmem),
        scratch_shapes=[
            pltpu.VMEM((FAR, count, width, half), F32),
            pltpu.VMEM((LEADS, 2, width, half), F32),
            pltpu.VMEM((2, width, width), F32),
            pltpu.VMEM((2, width, width), F32),
            pltpu.VMEM((STEPS + 2, width, (STEPS + 1) * width), BF16),
            pltpu.VMEM((STEPS + 2, width, (STEPS + 1) * width), BF16),
            pltpu.VMEM((width, (STEPS + 1) * width), F32),
            pltpu.VMEM((width, (STEPS + 1) * width), F32),
            dma((planes,)),
            dma((depth,)),
            dma((LEADS,)),
            dma((2, 3)),
            dma((2, 3)),
            dma((2, 3)),
            dma((2, 3)),
            dma((2,)),
            dma((2,)),
            dma((REACH * DOWN,)),
            dma((REACH * DOWN,)),
            dma(((REACH + 1) * ups,)),
            dma(((REACH + 1) * ups,)),
        ],
        compiler_params=pltpu.CompilerParams(
            collective_id=0, has_side_effects=True, vmem_limit_bytes=40 * 1024 * 1024
        ),
        cost_estimate=pl.CostEstimate(flops=20_000_000_000, bytes_accessed=6 * 1024 * 1024, transcendentals=0),
    )(local)
    return factor[:, :, None], second[:, None]


def solution(mesh, depth=DEPTH, side=SIDE):
    n = mesh.shape["blk"]
    return jax.shard_map(
        functools.partial(body, n, depth, side),
        mesh=mesh,
        in_specs=(P(None, "blk", None, "ch"),),
        out_specs=(P(None, None, "blk", None, "ch"), P(None, "blk", None, "ch")),
        check_vma=False,
    )
```

```python
import functools

import jax
import jax.numpy as jnp
from jax import lax
from jax.experimental import pallas as pl
from jax.experimental.pallas import tpu as pltpu
from jax.sharding import PartitionSpec as P

MESH = pl.DeviceIdType.MESH
F32, BF16 = jnp.float32, jnp.bfloat16

STEPS = 3
OWN_AT = (([0, 1], []), ([2, 3, 4], [0, 1, 2]), ([], []), ([], []))
AT_START = (([], []), ([10], [4]), ([13], [7]))
AFTER_INVERSE = (([8], [2]), ([11], [5]), ([14], [8]))
AFTER_ROOTS = (([9], [3]), ([12], [6]), ([], [9]))
LEADS = STEPS + 1
REACH = STEPS + 1
DEPTH = 8
SIDE = 4
DOWN = 5
FAR = REACH + 1
RISE = 3


def split(a):
    high = a.astype(BF16)
    return high, (a - high.astype(F32)).astype(BF16)


def dot_of_parts(left, right):
    (lh, ll), (rh, rl) = left, right
    return jnp.dot(
        jnp.concatenate([lh, ll, lh], axis=1),
        jnp.concatenate([rh, rh, rl], axis=0),
        preferred_element_type=F32,
    )


def mul(left, right):
    return dot_of_parts(split(left), split(right))


def wait_for(ref, sem):
    pltpu.make_async_copy(ref, ref, sem).wait()


def kernel(n, depth, side, x_ref, factor_ref, second_ref, halo, lead, why, zed, coef_high, coef_low, a_ref, c_ref,
           scatter_send, z_send, piece_recv, y_send, y_recv, row_send, row_recv, sib_send, sib_recv,
           down_send, down_recv, up_send, up_recv):
    width = x_ref.shape[1]
    count = x_ref.shape[0]
    half = x_ref.shape[2]
    ups = count - DOWN
    b, ch = lax.axis_index("blk"), lax.axis_index("ch")
    planes = n // depth
    rows = width // planes
    p, z = lax.div(b, depth), lax.rem(b, depth)
    below, above = lax.rem(b + n - 1, n), lax.rem(b + 1, n)
    first_stop = p * depth + lax.rem(z + RISE, depth)
    held_from = p * depth + lax.rem(z + depth - RISE, depth)
    second_stop = lax.rem(held_from + n - REACH, n)
    sender = lax.rem(b + REACH, n)
    second_sender = lax.div(sender, depth) * depth + lax.rem(lax.rem(sender, depth) + RISE, depth)

    across = planes // side
    row, column = lax.div(p, side), lax.rem(p, side)

    def in_row(i):
        return {"blk": (row * side + lax.rem(column + i, side)) * depth + z}

    def in_column(i):
        return {"blk": (lax.rem(row + i, across) * side + column) * depth + z}

    def in_line(i):
        return {"blk": p * depth + lax.rem(z + i, depth)}

    sibling = {"ch": 1 - ch}

    def each(start, stop, body):
        def run(i, carry):
            body(i)
            return carry

        lax.fori_loop(start, stop, run, 0)

    def push(src, dst, send, recv, to):
        return pltpu.make_async_remote_copy(
            src_ref=src, dst_ref=dst, send_sem=send, recv_sem=recv, device_id=to, device_id_type=MESH
        )

    barrier = pltpu.get_barrier_semaphore()

    def greet(to):
        pl.semaphore_signal(barrier, inc=1, device_id=to, device_id_type=MESH)

    for to in (above, below, held_from, second_sender):
        greet({"blk": to})
    greet(sibling)
    for i in range(1, side):
        greet(in_row(i))
    for i in range(1, across):
        greet(in_column(i))
    for item in range(LEADS):

        @pl.when(z != item)
        def _():
            greet({"blk": p * depth + item})

    @pl.when((z < LEADS) & (p > 0))
    def _():
        greet({"blk": z})

    owner, forwards = (b < LEADS).astype(jnp.int32), (z < LEADS).astype(jnp.int32)
    pl.semaphore_wait(
        barrier, 5 + (side - 1) + (across - 1) + forwards * (depth - 1) + owner * (planes - 1)
    )

    def piece(item, i):
        return lead.at[item, ch, pl.ds(pl.multiple_of(i * rows, rows), rows)]

    def own_piece(i):
        return x_ref.at[0, pl.ds(pl.multiple_of(i * rows, rows), rows)]

    def scatter_copy(i):
        return push(own_piece(i), piece(b, i), scatter_send.at[i], piece_recv.at[b], {"blk": i * depth + b})

    def line_copy(item, i):
        return push(piece(item, p), piece(item, p), z_send.at[i], piece_recv.at[item], in_line(i))

    groups = ((0, 1), (1, LEADS - 1))

    def lead_rows(g, start, size):
        return lead.at[pl.ds(*groups[g]), ch, pl.ds(start, size)]

    def ring(g, size, place, region, neighbour, sends, recvs):
        def copy(k, part, by):
            return push(region(g, part), region(g, part), sends.at[g, k], recvs.at[g, k], neighbour(by))

        behind = [lax.rem(place + size - i, size) for i in range(size)]
        copies = [copy(i, behind[i], 1) for i in range(size - 1)]

        def first():
            for c in copies[:1]:
                c.start()

        def arrived(i):
            wait_for(region(g, behind[i]), recvs.at[g, i - 1])
            for c in copies[i : i + 1]:
                c.start()

        def second():
            if size > 1:
                arrived(1)

        def third():
            for i in range(2, size):
                arrived(i)

        def sent():
            for c in copies:
                c.wait_send()

        return first, second, third, sent

    def row_region(g, i):
        return lead_rows(g, pl.multiple_of((row * side + i) * rows, rows), rows)

    def column_region(g, i):
        return lead_rows(g, pl.multiple_of(i * side * rows, side * rows), side * rows)

    row_rings = [ring(g, side, column, row_region, in_row, y_send, y_recv) for g in range(2)]
    column_rings = [ring(g, across, row, column_region, in_column, row_send, row_recv) for g in range(2)]

    def sibling_copy(g):
        part = lead.at[pl.ds(*groups[g]), ch]
        return push(part, part, sib_send.at[g], sib_recv.at[g], sibling)

    def complete(g):
        wait_for(lead.at[pl.ds(*groups[g]), 1 - ch], sib_recv.at[g])

    @pl.when(b < LEADS)
    def _():
        pltpu.make_async_copy(own_piece(0), piece(b, 0), piece_recv.at[b]).start()
        each(1, planes, lambda i: scatter_copy(i).start())

    def down_copy(t, src):
        s, r = lax.div(t, DOWN), lax.rem(t, DOWN)
        return push(src, halo.at[s, r], down_send.at[t], down_recv.at[t], {"blk": below})

    def up_copy(t, src, to):
        s, r = FAR - 1 - lax.div(t, ups), DOWN + lax.rem(t, ups)
        return push(src, halo.at[s, r], up_send.at[t], up_recv.at[t], {"blk": to})

    def down_source(t):
        return halo.at[lax.div(t, DOWN) - 1, lax.rem(t, DOWN)]

    def up_source(t):
        return halo.at[FAR - lax.div(t, ups), DOWN + lax.rem(t, ups)]

    n_down, n_up = REACH * DOWN, (REACH + 1) * ups

    def down_arrived(t):
        wait_for(halo.at[lax.div(t, DOWN), lax.rem(t, DOWN)], down_recv.at[t])

    def up_arrived(t):
        wait_for(halo.at[FAR - 1 - lax.div(t, ups), DOWN + lax.rem(t, ups)], up_recv.at[t])

    def relay(downs=(), upwards=()):
        for t in downs:
            down_arrived(t)
            down_copy(t + DOWN, down_source(t + DOWN)).start()
        for t in upwards:
            up_arrived(t)
            up_copy(t + ups, up_source(t + ups), second_stop if t < ups else above).start()

    def own(downs=(), upwards=()):
        for t in downs:
            down_copy(t, x_ref.at[t]).start()
        for t in upwards:
            up_copy(t, x_ref.at[DOWN + t], first_stop).start()

    def pass_pieces(g):
        first, size = groups[g]
        for item in range(first, first + size):

            @pl.when(z != item)
            def _():
                wait_for(piece(item, p), piece_recv.at[item])

        row_rings[g][0]()

    own(*OWN_AT[0])

    @pl.when(z < LEADS)
    def _():
        wait_for(piece(z, p), piece_recv.at[z])
        each(1, depth, lambda i: line_copy(z, i).start())

    own(*OWN_AT[1])
    pass_pieces(0)
    pass_pieces(1)
    own(*OWN_AT[2])
    row_rings[0][1]()
    row_rings[1][1]()
    for g in range(2):
        row_rings[g][2]()
        column_rings[g][0]()
    own(*OWN_AT[3])
    column_rings[0][1]()
    column_rings[1][1]()
    relay([0, 1])
    column_rings[0][2]()
    sibling_copy(0).start()
    relay([2])
    column_rings[1][2]()
    sibling_copy(1).start()
    relay([3])

    def lead_block(item):
        return jnp.concatenate([lead[item, 0], lead[item, 1]], axis=1)

    eye = (
        lax.broadcasted_iota(jnp.int32, (width, width), 0) == lax.broadcasted_iota(jnp.int32, (width, width), 1)
    ).astype(F32)

    def scale_of(a):
        return jnp.max(jnp.sum(jnp.abs(a), axis=0, keepdims=True), axis=1, keepdims=True)

    def roots(matrices, sweeps):
        kept = range(len(matrices))
        scales = [scale_of(a) for a in matrices]
        starts = [a * (1.0 / s) for a, s in zip(matrices, scales)]
        middles = [1.5 * eye - 0.5 * y for y in starts]
        firsts = [mul(y, t) for y, t in zip(starts, middles)]
        for i in kept:
            zed[i] = middles[i]
            why[i] = firsts[i]

        def sweep(k, carry):
            ys = [split(why[i]) for i in kept]
            zs = [split(zed[i]) for i in kept]
            ts = [split(1.5 * eye - 0.5 * dot_of_parts(zs[i], ys[i])) for i in kept]
            new_ys = [dot_of_parts(ys[i], ts[i]) for i in kept]
            new_zs = [dot_of_parts(ts[i], zs[i]) for i in kept]
            for i in kept:
                why[i] = new_ys[i]
                zed[i] = new_zs[i]
            return carry

        lax.fori_loop(0, sweeps - 1, sweep, 0)
        return scales

    def cols(j, k=1):
        return pl.ds(j * width, k * width)

    def keep_coefficients(o, value, terms):
        high, low = split(value)
        coef_high[o, :, : terms * width] = high
        coef_low[o, :, : terms * width] = low

    complete(0)
    relay([4])
    (s,) = roots([lead_block(0)], 6)
    relay([5, 6], [0])
    root = jnp.sqrt(s)
    w = zed[0] * (1.0 / root)
    x0 = why[0] * root
    complete(1)
    rest = mul(w, jnp.concatenate([lead_block(item) for item in range(1, LEADS)], axis=1))
    uppers = [x0] + [rest[:, i * width : (i + 1) * width] for i in range(LEADS - 1)]
    lowers = uppers[1:]
    keep_coefficients(0, w, 1)
    a_ref[:, cols(0)] = w
    c_ref[:, cols(0)] = w
    relay([7], [1])

    for k in range(STEPS):
        terms = k + 1
        x, y = uppers[0], lowers[0]
        relay(*AT_START[k])
        both = mul(x, jnp.concatenate([x.T, y.T], axis=1))
        gram, cross = both[:, :width], both[:, width:]
        s = 1.0 / scale_of(gram)
        power = eye - gram * s
        total = cross * s
        for i in range(4):
            both = mul(power, jnp.concatenate([power, total], axis=1))
            power, total = both[:, :width], total + both[:, width:]
        kt = total + mul(power, total)
        kk = kt.T
        kt_parts, kk_parts = split(kt), split(kk)
        relay(*AFTER_INVERSE[k])
        scales = roots([eye - dot_of_parts(kt_parts, kk_parts), eye - dot_of_parts(kk_parts, kt_parts)], 5)
        relay(*AFTER_ROOTS[k])
        first = zed[0] * (1.0 / jnp.sqrt(scales[0]))
        second = zed[1] * (1.0 / jnp.sqrt(scales[1]))
        first_parts, second_parts = split(first), split(second)
        more = STEPS - 1 - k
        if more > 0:
            d = jnp.concatenate(uppers[:more], axis=1) - dot_of_parts(
                kt_parts, split(jnp.concatenate(lowers[:more], axis=1)))
            e = jnp.concatenate(lowers[1 : more + 1], axis=1) - dot_of_parts(
                kk_parts, split(jnp.concatenate(uppers[1 : more + 1], axis=1)))
            d = dot_of_parts(first_parts, split(d))
            e = dot_of_parts(second_parts, split(e))
            uppers = [d[:, i * width : (i + 1) * width] for i in range(more)]
            lowers = [e[:, i * width : (i + 1) * width] for i in range(more)]
        a, c = a_ref[:, cols(0, terms)], c_ref[:, cols(0, terms)]
        ktc = dot_of_parts(kt_parts, split(c))
        kka = dot_of_parts(kk_parts, split(a))
        none = jnp.zeros((width, width), F32)
        d = jnp.concatenate([a, none], axis=1) - jnp.concatenate([none, ktc], axis=1)
        e = jnp.concatenate([none, c], axis=1) - jnp.concatenate([kka, none], axis=1)
        a = dot_of_parts(first_parts, split(d))
        c = dot_of_parts(second_parts, split(e))
        a_ref[:, cols(0, terms + 1)] = a
        c_ref[:, cols(0, terms + 1)] = c
        keep_coefficients(k + 1, a, terms + 1)
        if k == STEPS - 1:
            keep_coefficients(STEPS + 1, c, terms + 1)

    def data(j, q):
        wrapped = (b + j >= n).astype(jnp.int32)
        blocks = []
        for i in range(2):
            r = 2 * q + i
            if j == 0:
                blocks.append(x_ref[r])
            else:
                block = halo[j - 1, jnp.minimum(r + wrapped, count - 1)]
                blocks.append(jnp.where(r + wrapped < count, block, jnp.zeros_like(block)))
        return split(jnp.concatenate(blocks, axis=1))

    def terms_of(o, q, slots, add):
        shift = 1 if o > STEPS else 0
        parts = [data(j, q) for j in slots]
        left = [
            jnp.concatenate([ref[o, :, (j - shift) * width : (j - shift + 1) * width] for j in slots], axis=1)
            for ref in (coef_high, coef_low)
        ]
        right = [jnp.concatenate([part[i] for part in parts], axis=0) for i in range(2)]
        value = dot_of_parts(left, right)
        for i in range(2):
            cut = value[:, i * half : (i + 1) * half]
            r = 2 * q + i
            if o > STEPS:
                second_ref[r] = second_ref[r] + cut if add else cut
            else:
                factor_ref[o, r] = factor_ref[o, r] + cut if add else cut

    def own_row(q):
        terms_of(0, q, [0], False)

    def near_rows(q):
        for o in range(1, STEPS + 1):
            terms_of(o, q, list(range(o + 1)), False)
        terms_of(STEPS + 1, q, [1, 2, 3], False)

    def near_last(q):
        terms_of(STEPS + 1, q, [4], True)

    def far_rows(q, row):
        terms_of(2, q, [0, 2], False)
        terms_of(3, q, [0, 2, 3], False)
        terms_of(4, q, row, False)

    def far_last(q, row):
        terms_of(1, q, [0, 1], False)
        for o in range(2, STEPS + 1):
            terms_of(o, q, [1], True)
        terms_of(STEPS + 1, q, row, True)

    relay([], [10])
    each(0, 4, own_row)
    relay([], [11])
    each(0, 2, near_rows)
    far_rows(2, [2, 3])
    far_rows(3, [2, 3, 4])
    each(n_down - DOWN, n_down, down_arrived)
    each(0, 2, near_last)
    each(n_up - ups, n_up, up_arrived)
    far_last(2, [1, 4])
    far_last(3, [1])

    @pl.when(b < LEADS)
    def _():
        each(1, planes, lambda i: scatter_copy(i).wait_send())
        each(1, depth, lambda i: line_copy(b, i).wait_send())

    @pl.when((b >= LEADS) & (z < LEADS))
    def _():
        each(1, depth, lambda i: line_copy(z, i).wait_send())

    for g in range(len(groups)):
        row_rings[g][3]()
        column_rings[g][3]()
        sibling_copy(g).wait_send()
    each(0, n_down, lambda t: down_copy(t, x_ref.at[0]).wait_send())
    each(0, n_up, lambda t: up_copy(t, x_ref.at[0], above).wait_send())


def body(n, depth, side, blocks):
    local = blocks[:, 0]
    count, width, half = local.shape
    ups = count - DOWN
    planes = n // depth
    dma = pltpu.SemaphoreType.DMA
    in_vmem = pl.BlockSpec(memory_space=pltpu.VMEM)
    factor, second = pl.pallas_call(
        functools.partial(kernel, n, depth, side),
        out_shape=(
            jax.ShapeDtypeStruct((STEPS + 1, count, width, half), F32),
            jax.ShapeDtypeStruct((count, width, half), F32),
        ),
        in_specs=[in_vmem],
        out_specs=(in_vmem, in_vmem),
        scratch_shapes=[
            pltpu.VMEM((FAR, count, width, half), F32),
            pltpu.VMEM((LEADS, 2, width, half), F32),
            pltpu.VMEM((2, width, width), F32),
            pltpu.VMEM((2, width, width), F32),
            pltpu.VMEM((STEPS + 2, width, (STEPS + 1) * width), BF16),
            pltpu.VMEM((STEPS + 2, width, (STEPS + 1) * width), BF16),
            pltpu.VMEM((width, (STEPS + 1) * width), F32),
            pltpu.VMEM((width, (STEPS + 1) * width), F32),
            dma((planes,)),
            dma((depth,)),
            dma((LEADS,)),
            dma((2, 3)),
            dma((2, 3)),
            dma((2, 3)),
            dma((2, 3)),
            dma((2,)),
            dma((2,)),
            dma((REACH * DOWN,)),
            dma((REACH * DOWN,)),
            dma(((REACH + 1) * ups,)),
            dma(((REACH + 1) * ups,)),
        ],
        compiler_params=pltpu.CompilerParams(
            collective_id=0, has_side_effects=True, vmem_limit_bytes=40 * 1024 * 1024
        ),
        cost_estimate=pl.CostEstimate(flops=20_000_000_000, bytes_accessed=6 * 1024 * 1024, transcendentals=0),
    )(local)
    return factor[:, :, None], second[:, None]


def solution(mesh, depth=DEPTH, side=SIDE):
    n = mesh.shape["blk"]
    return jax.shard_map(
        functools.partial(body, n, depth, side),
        mesh=mesh,
        in_specs=(P(None, "blk", None, "ch"),),
        out_specs=(P(None, None, "blk", None, "ch"), P(None, "blk", None, "ch")),
        check_vma=False,
    )
```
